256 devices in a mesh: ep: 16 (over z, core), sp: 16 (over x, y).
Axes of the slice: x: 4, y: 4, z: 8, core: 2. Of those that a mesh axis runs over, the one named last changes fastest.
Arguments:
- queries: bfloat16 [65536, 2048], P(('ep', 'sp')), may hold values from -6 to 6
- keys: bfloat16 [65536, 2048], P(('ep', 'sp')), may hold values from -6 to 6
- values: bfloat16 [65536, 2048], P(('ep', 'sp')), may hold values from -6 to 6
- residual: bfloat16 [65536, 2048], P('ep', 'sp'), may hold values from -6 to 6
- cotangent: bfloat16 [65536, 2048], P('ep', 'sp'), may hold values from -1.5 to 1.5
- gate_proj: bfloat16 [16, 2048, 4096], P('ep', None, 'sp'), may hold values from -0.1875 to 0.1875
- up_proj: bfloat16 [16, 2048, 4096], P('ep', None, 'sp'), may hold values from -0.125 to 0.125
- down_proj: bfloat16 [16, 4096, 2048], P('ep', 'sp'), may hold values from -0.125 to 0.125
- chosen: int32 [16, 16, 32], P('ep'), may hold values from 0 to 4095, as said below
- counts: int32 [16, 16], P('ep'), may hold values from 0 to 32, as said below
- route_weight: float32 [16, 16, 32], P('ep'), may hold values from 0.5 to 3
Outputs:
- block_out: bfloat16 [65536, 2048], P('ep', 'sp')
- grad_hidden: bfloat16 [65536, 2048], P('ep', 'sp')
- grad_down: bfloat16 [16, 4096, 2048], P('ep', 'sp')
The draws below stay inside these ranges and needn't reach their ends.
Inputs may be any that keep to these rules, and one draw needn't show every extreme that they name: `chosen`: the 32 positions of one list (one image, one expert) are distinct. The live slots of a list are its first counts[a, e]; in every draw some expert has all 32 slots live in every image.
All inputs are finite; a program needn't handle non-finite values.
Results may differ from the reference program's by a relative error of at most 0.014.
Values may be sent and summed in bfloat16 or wider, within the bound.
No kernel may reach another device: no remote copies, remote signals or barrier semaphores. Data moves between devices by JAX's collectives and lax.ppermute only.
A program may use at most 64 MiB of HBM per device.

```python
import math
import jax
import jax.numpy as jnp
from jax import lax

HEADS = 16
HD = 128
FF = 4096
SLOTS = 32
D = 2048
LENGTH = 4096
TOKENS = 65536
EXPERTS = 16
N_EP = 16
N_SP = 16


def draw_queries(key, part):
    key = jax.random.fold_in(key, 3)
    drawn = jnp.clip(1.6 * jax.random.normal(key, (TOKENS, D), jnp.float32), -6.0, 6.0)
    return drawn.astype(jnp.bfloat16)


def draw_keys(key, part):
    key = jax.random.fold_in(key, 4)
    drawn = jnp.clip(1.6 * jax.random.normal(key, (TOKENS, D), jnp.float32), -6.0, 6.0)
    return drawn.astype(jnp.bfloat16)


def place_value(row, value, slot):
    present = row == value
    previous = row[slot]
    row = jnp.where(present, previous, row)
    return row.at[slot].set(value)


def draw_chosen(key, part):
    key = jax.random.fold_in(key, 5)
    list_keys = jax.random.split(key, N_EP * EXPERTS + 1)

    def one_list(list_key):
        return jax.random.permutation(list_key, LENGTH)[:SLOTS].astype(jnp.int32)
    lists = jax.vmap(one_list)(list_keys[1:]).reshape(N_EP, EXPERTS, SLOTS)
    key_expert, key_top, key_low = jax.random.split(list_keys[0], 3)
    forced = jax.random.randint(key_expert, (N_EP,), 0, EXPERTS).astype(jnp.int32)
    slot_top = jax.random.randint(key_top, (N_EP,), 0, SLOTS).astype(jnp.int32)
    slot_low = ((slot_top + 1 + jax.random.randint(key_low, (N_EP,), 0, SLOTS - 1)) % SLOTS).astype(jnp.int32)
    images = jnp.arange(N_EP)
    picked = lists[images, forced]
    picked = jax.vmap(place_value, in_axes=(0, None, 0))(picked, jnp.int32(LENGTH - 1), slot_top)
    picked = jax.vmap(place_value, in_axes=(0, None, 0))(picked, jnp.int32(0), slot_low)
    return lists.at[images, forced].set(picked).astype(jnp.int32)


def draw_counts(key, part):
    key = jax.random.fold_in(key, 7)
    key_first, key_second, key_hot = jax.random.split(key, 3)
    first = jax.random.randint(key_first, (N_EP, EXPERTS), 0, SLOTS + 1)
    second = jax.random.randint(key_second, (N_EP, EXPERTS), 0, SLOTS + 1)
    hottest = jax.random.randint(key_hot, (), 0, EXPERTS)
    lower = jnp.minimum(first, second)
    return jnp.where(jnp.arange(EXPERTS)[None, :] == hottest, SLOTS, lower).astype(jnp.int32)


def raised(entries, rng, source, target, shards_of, factor):
    owner, partner = [(jnp.arange(entries.shape[axis_at]) // (entries.shape[axis_at] // shards_of)).reshape([-1 if axis == axis_at else 1 for axis in range(entries.ndim)]) for axis_at in (source, target)]
    chosen = jax.random.permutation(rng, shards_of)[partner]
    strong = (owner == chosen) | (owner == (partner + shards_of // 2) % shards_of)
    return jnp.where(strong, factor * entries, entries)


def block_scale(own_key, shape, shards, least, top_value):
    level, own = 1.0, jax.random.fold_in(own_key, 6)
    for position, shards_of in shards:
        draws = jnp.exp(jax.random.uniform(jax.random.fold_in(own, position), (shards_of,), jnp.float32, least / len(shards), top_value / len(shards)))
        level = level * jnp.repeat(draws, shape[position] // shards_of).reshape([-1 if axis == position else 1 for axis in range(len(shape))])
    return level


def bell_draw(stream_key, shape, width, limit, shards=(), held_as=jnp.bfloat16):
    drawn = jax.random.normal(stream_key, shape, jnp.float32) * width
    if len(shards) > 0:
        drawn = block_scale(stream_key, shape, shards, -0.22, 0.18) * drawn
    return jnp.clip(drawn, min=-limit, max=limit).astype(held_as)


def gaussian_with(stream_key, shape, scale, bound, cuts, heavy, held_as=jnp.bfloat16):
    array = scale * jax.random.normal(stream_key, shape, jnp.float32)
    if cuts:
        array = array * block_scale(stream_key, shape, cuts, -0.22, 0.18)
    return jnp.clip(raised(array, jax.random.fold_in(stream_key, 3), *heavy), -bound, bound).astype(held_as)


def setup_inputs(seed: int = 0) -> dict:
    key_of = jax.random.split(jax.random.key(seed), 12)
    queries = draw_queries(jax.random.fold_in(key_of[11], 71), 0)
    keys = draw_keys(jax.random.fold_in(key_of[11], 71), 0)
    values = bell_draw(key_of[2], (TOKENS, D), 1.0, 6.0, ((0, 256),))
    residual = bell_draw(key_of[3], (TOKENS, D), 1.0, 6.0, ((0, 16), (1, 16)))
    cotangent = bell_draw(key_of[4], (TOKENS, D), 0.25, 1.5, ((0, 16), (1, 16)))
    gate_proj = gaussian_with(key_of[5], (EXPERTS, D, FF), D ** -0.5, 0.1875, ((0, 16), (2, 16)), (2, 1, 16, 2.0))
    up_proj = bell_draw(key_of[6], (EXPERTS, D, FF), D ** -0.5, 0.125, ((0, 16), (2, 16)))
    down_proj = gaussian_with(key_of[7], (EXPERTS, FF, D), FF ** -0.5, 0.125, ((0, 16), (1, 16)), (1, 2, 16, 2.0))
    chosen = draw_chosen(jax.random.fold_in(key_of[11], 71), 0)
    counts = draw_counts(jax.random.fold_in(key_of[11], 71), 0)
    route_weight = jnp.clip(jnp.exp(math.log(3.0) - 1.7917595 * jax.random.uniform(key_of[10], (N_EP, EXPERTS, SLOTS), jnp.float32) ** block_scale(key_of[10], (N_EP, EXPERTS, SLOTS), ((0, 16),), -0.2, 0.2)), 0.5, 3.0)
    return {"queries": queries, "keys": keys, "values": values, "residual": residual, "cotangent": cotangent, "gate_proj": gate_proj, "up_proj": up_proj, "down_proj": down_proj, "chosen": chosen, "counts": counts, "route_weight": route_weight}


def one_head(trio):
    query, key, value = trio
    scores = jnp.dot(query, key.T, preferred_element_type=jnp.float32) * (HD ** -0.5)
    top = jnp.max(scores, axis=-1, keepdims=True)
    expd = jnp.exp(scores - top)
    probs = (expd / jnp.sum(expd, axis=-1, keepdims=True)).astype(jnp.bfloat16)
    return jnp.dot(probs, value, preferred_element_type=jnp.float32).astype(jnp.bfloat16)


def image_attention(trio):
    split_heads = [part.reshape(LENGTH, HEADS, HD).transpose(1, 0, 2) for part in trio]
    heads_out = lax.map(one_head, tuple(split_heads))
    return heads_out.transpose(1, 0, 2).reshape(LENGTH, D)


def settle(partials):
    rounded = lax.optimization_barrier(partials.astype(jnp.bfloat16))
    return jnp.sum(rounded.astype(jnp.float32), axis=0).astype(jnp.bfloat16)


def reference(queries, keys, values, residual, cotangent, gate_proj, up_proj, down_proj, chosen, counts, route_weight):
    trio = (queries.reshape(N_EP, LENGTH, D), keys.reshape(N_EP, LENGTH, D), values.reshape(N_EP, LENGTH, D))
    attended = lax.map(image_attention, trio).reshape(TOKENS, D)
    hidden = (residual.astype(jnp.float32) + attended.astype(jnp.float32)).astype(jnp.bfloat16)
    live_slot = jnp.arange(SLOTS, dtype=jnp.int32)[None, None, :] < counts[:, :, None]
    weight = jnp.where(live_slot, route_weight, jnp.float32(0.0)).astype(jnp.float32)
    tokens_at = (chosen + (jnp.arange(N_EP, dtype=jnp.int32) * LENGTH)[:, None, None]).astype(jnp.int32)
    tangents_all = (cotangent[tokens_at].astype(jnp.float32) * weight[..., None]).astype(jnp.bfloat16)
    row_total = N_EP * SLOTS
    block_width = FF // N_SP

    def one_expert(pack):
        places, tangent_rows, gate_w, up_w, down_w = pack
        rows = hidden[places.reshape(-1)]
        gate_pre = jnp.dot(rows, gate_w, preferred_element_type=jnp.float32)
        up_pre = jnp.dot(rows, up_w, preferred_element_type=jnp.float32)
        act = (jax.nn.silu(gate_pre) * up_pre).astype(jnp.bfloat16)
        act_blocks = act.astype(jnp.float32).reshape(row_total, N_SP, block_width)
        down_blocks = down_w.astype(jnp.float32).reshape(N_SP, block_width, D)
        expert_out = settle(jnp.einsum("rsf,sfd->srd", act_blocks, down_blocks))
        tangents = tangent_rows.reshape(row_total, D)
        grad_down = jnp.dot(act.T, tangents, preferred_element_type=jnp.float32).astype(jnp.bfloat16)
        d_act = jnp.dot(tangents, down_w.T, preferred_element_type=jnp.float32)
        sig_gate = jax.nn.sigmoid(gate_pre)
        d_gate = (d_act * up_pre * sig_gate * (1.0 + gate_pre * (1.0 - sig_gate))).astype(jnp.bfloat16)
        d_up = (d_act * jax.nn.silu(gate_pre)).astype(jnp.bfloat16)
        gate_blocks = gate_w.astype(jnp.float32).reshape(D, N_SP, block_width)
        up_blocks = up_w.astype(jnp.float32).reshape(D, N_SP, block_width)
        d_parts = jnp.einsum("rsf,dsf->srd", d_gate.astype(jnp.float32).reshape(row_total, N_SP, block_width), gate_blocks)
        d_parts = d_parts + jnp.einsum("rsf,dsf->srd", d_up.astype(jnp.float32).reshape(row_total, N_SP, block_width), up_blocks)
        d_rows = settle(d_parts)
        return expert_out, d_rows, grad_down

    places_all = tokens_at.transpose(1, 0, 2)
    pack = (places_all, tangents_all.transpose(1, 0, 2, 3), gate_proj, up_proj, down_proj)
    expert_out, d_rows, grad_down = lax.map(one_expert, pack)
    flat_places = places_all.reshape(-1)
    flat_weight = weight.transpose(1, 0, 2).reshape(-1)
    combined = jnp.zeros((TOKENS, D), jnp.float32).at[flat_places].add(expert_out.reshape(-1, D).astype(jnp.float32) * flat_weight[:, None])
    block_out = (hidden.astype(jnp.float32) + combined).astype(jnp.bfloat16)
    row_grads = jnp.zeros((TOKENS, D), jnp.float32).at[flat_places].add(d_rows.reshape(-1, D).astype(jnp.float32))
    grad_hidden = (cotangent.astype(jnp.float32) + row_grads).astype(jnp.bfloat16)
    return block_out, grad_hidden, grad_down
```

```python
import functools

import jax
import jax.numpy as jnp
from jax import lax
from jax.experimental import pallas as pl
from jax.experimental.pallas import tpu as pltpu
from jax.sharding import PartitionSpec as P

HD = 128
SLOTS = 32
SIDE = 4
LOG2E = 1.4426950408889634
VMEM_LIMIT = 48 * 1024 * 1024
BIG_VMEM = 60 * 1024 * 1024
SAFE_EXPONENT = 110.0
F32 = jnp.float32
BF16 = jnp.bfloat16
OVER_LAST = (((1,), (1,)), ((), ()))


def params(limit=VMEM_LIMIT):
    return pltpu.CompilerParams(vmem_limit_bytes=limit)


def pack_kernel(q_ref, k_ref, v_ref, out_ref):
    rows, width = q_ref.shape
    for h in range(width // HD):
        here = slice(h * HD, (h + 1) * HD)
        out_ref[h, 0:rows, :] = q_ref[:, here]
        out_ref[h, rows : 2 * rows, :] = k_ref[:, here]
        out_ref[h, 2 * rows : 3 * rows, :] = v_ref[:, here]


def pack(queries, keys, values):
    rows, width = queries.shape
    heads = width // HD
    steps = 4
    columns = pl.BlockSpec((rows, width // steps), lambda h: (0, h))
    return pl.pallas_call(
        pack_kernel,
        grid=(steps,),
        in_specs=[columns] * 3,
        out_specs=pl.BlockSpec((heads // steps, 3 * rows, HD), lambda h: (h, 0, 0)),
        out_shape=jax.ShapeDtypeStruct((heads, 3 * rows, HD), BF16),
        compiler_params=params(BIG_VMEM),
        name="pack_qkv",
    )(queries, keys, values)


def attention_kernel(rows, q_ref, res_ref, qkv_ref, out_ref, peak_ref):
    sources = qkv_ref.shape[0]
    block = res_ref.shape[0]
    part = min(256, block)
    scale = HD**-0.5 * LOG2E

    @pl.when(pl.program_id(0) == 0)
    def _():
        peak = jnp.zeros((rows, HD), F32)
        for s in range(sources):
            key = qkv_ref[s, rows : 2 * rows, :].astype(F32)
            square = (key * key).astype(BF16)
            peak = jnp.maximum(
                peak, jnp.dot(square, jnp.ones((HD, HD), BF16), preferred_element_type=F32)
            )
        peak_ref[0] = jnp.max(peak)

    query = q_ref[...].reshape(block, HD)
    wide_query = query.astype(F32)
    longest = jnp.max(jnp.sum(wide_query * wide_query, axis=1, keepdims=True))
    small = longest * peak_ref[0] * (1.02 * scale * scale) <= SAFE_EXPONENT * SAFE_EXPONENT

    def scores_of(here, s):
        return (
            lax.dot_general(
                query[here], qkv_ref[s, rows : 2 * rows, :], OVER_LAST, preferred_element_type=F32
            )
            * scale
        )

    def finish(here, total, norm):
        norm = jnp.sum(norm, axis=1, keepdims=True)
        attended = (total / norm).astype(BF16)
        out_ref[here, :] = (res_ref[here, :].astype(F32) + attended.astype(F32)).astype(BF16)

    def add_up(here, shift):
        total = jnp.zeros((part, HD), F32)
        norm = jnp.zeros((part, HD), F32)
        for s in range(sources):
            scores = scores_of(here, s)
            probs = jnp.exp2(scores if shift is None else scores - shift)
            for c in range(rows // HD):
                norm = norm + probs[:, c * HD : (c + 1) * HD]
            total = total + jnp.dot(
                probs.astype(BF16), qkv_ref[s, 2 * rows : 3 * rows, :], preferred_element_type=F32
            )
        finish(here, total, norm)

    @pl.when(small)
    def _():
        for p in range(block // part):
            add_up(slice(p * part, (p + 1) * part), None)

    @pl.when(jnp.logical_not(small))
    def _():
        for p in range(block // part):
            here = slice(p * part, (p + 1) * part)
            top = jnp.full((part, 1), -jnp.inf, F32)
            for s in range(sources):
                top = jnp.maximum(top, jnp.max(scores_of(here, s), axis=1, keepdims=True))
            add_up(here, top)


def attention(queries, query_spec, residual, residual_first, total, qkv, block, name):
    sources, rows3, _ = qkv.shape
    rows = rows3 // 3
    length = sources * rows
    return pl.pallas_call(
        functools.partial(attention_kernel, rows),
        grid=(total // block,),
        in_specs=[
            query_spec,
            pl.BlockSpec((block, HD), lambda i: (i + residual_first, 0)),
            pl.BlockSpec((sources, rows3, HD), lambda i: (0, 0, 0)),
        ],
        out_specs=pl.BlockSpec((block, HD), lambda i: (i, 0)),
        out_shape=jax.ShapeDtypeStruct((total, HD), BF16),
        scratch_shapes=[pltpu.SMEM((1,), F32)],
        compiler_params=params(),
        cost_estimate=pl.CostEstimate(
            flops=8 * total * length * HD,
            bytes_accessed=4 * total * HD * 2 + qkv.size * 2,
            transcendentals=total * length,
        ),
        name=name,
    )(queries, residual, qkv)


def wide_rows(ref):
    return jnp.concatenate([ref[c] for c in range(ref.shape[0])], axis=1)


def tangent_kernel(tan_ref, down_ref, d_act_ref):
    d_act_ref[...] = lax.dot_general(
        wide_rows(tan_ref), down_ref[...], OVER_LAST, preferred_element_type=F32
    )


def tangent_product(tangent, down):
    blocks, total, width = tangent.shape
    hidden = down.shape[0]
    return pl.pallas_call(
        tangent_kernel,
        out_shape=jax.ShapeDtypeStruct((total, hidden), F32),
        compiler_params=params(),
        cost_estimate=pl.CostEstimate(
            flops=2 * total * hidden * blocks * width,
            bytes_accessed=2 * tangent.size + 2 * down.size + 4 * total * hidden,
            transcendentals=0,
        ),
        name="tangent_product",
    )(tangent, down)


def expert_kernel(
    me_ref, x_ref, d_act_ref, gate_ref, up_ref, down_ref, act_ref, out_ref, *grad_refs
):
    rows = wide_rows(x_ref)
    gate_pre = jnp.dot(rows, gate_ref[...], preferred_element_type=F32)
    up_pre = jnp.dot(rows, up_ref[...], preferred_element_type=F32)
    sig = jax.nn.sigmoid(gate_pre)
    silu = gate_pre * sig
    act = (silu * up_pre).astype(BF16)
    act_ref[...] = act
    d_act = d_act_ref[...]
    d_gate = (d_act * up_pre * sig * (1.0 + gate_pre * (1.0 - sig))).astype(BF16)
    d_up = (d_act * silu).astype(BF16)
    blocks, _, width = out_ref.shape
    side = len(grad_refs)
    for d in range(side):
        y = lax.rem(me_ref[0] + d, side)
        for x in range(0, side, 2):
            first = pl.ds(pl.multiple_of((x * side + y) * width, width), width)
            second = pl.ds(pl.multiple_of(((x + 1) * side + y) * width, width), width)
            gate = jnp.concatenate([gate_ref[first, :], gate_ref[second, :]], axis=0)
            up = jnp.concatenate([up_ref[first, :], up_ref[second, :]], axis=0)
            pair = lax.dot_general(d_gate, gate, OVER_LAST, preferred_element_type=F32)
            pair = pair + lax.dot_general(d_up, up, OVER_LAST, preferred_element_type=F32)
            pair = pair.astype(BF16)
            grad_refs[d][x] = pair[:, 0:width]
            grad_refs[d][x + 1] = pair[:, width : 2 * width]
    for c in range(0, blocks, 2):
        pair = jnp.dot(
            act, down_ref[:, c * width : (c + 2) * width], preferred_element_type=F32
        ).astype(BF16)
        out_ref[c] = pair[:, 0:width]
        out_ref[c + 1] = pair[:, width : 2 * width]


def expert(me, rows, d_act, gate, up, down, side):
    blocks, total, width = rows.shape
    hidden = gate.shape[1]
    quarter = jax.ShapeDtypeStruct((blocks // side, total, width), BF16)
    vmem = pl.BlockSpec(memory_space=pltpu.VMEM)
    return pl.pallas_call(
        expert_kernel,
        in_specs=[pl.BlockSpec(memory_space=pltpu.SMEM)] + [vmem] * 5,
        out_shape=(
            jax.ShapeDtypeStruct((total, hidden), BF16),
            jax.ShapeDtypeStruct((blocks, total, width), BF16),
        )
        + (quarter,) * side,
        compiler_params=params(),
        cost_estimate=pl.CostEstimate(
            flops=10 * total * hidden * blocks * width,
            bytes_accessed=6 * rows.size + 6 * gate.size + 6 * total * hidden,
            transcendentals=total * hidden,
        ),
        name="expert",
    )(me, rows, d_act, gate, up, down)


def down_grad_kernel(act_ref, tan_ref, grad_ref):
    grad_ref[...] = lax.dot_general(
        act_ref[...], wide_rows(tan_ref), (((0,), (0,)), ((), ())), preferred_element_type=F32
    ).astype(BF16)


def down_grad(act, tangent):
    blocks, total, width = tangent.shape
    hidden = act.shape[1]
    return pl.pallas_call(
        down_grad_kernel,
        out_shape=jax.ShapeDtypeStruct((hidden, blocks * width), BF16),
        compiler_params=params(),
        cost_estimate=pl.CostEstimate(
            flops=2 * total * hidden * blocks * width,
            bytes_accessed=2 * tangent.size + 2 * total * hidden + 2 * hidden * blocks * width,
            transcendentals=0,
        ),
        name="down_grad",
    )(act, tangent)


def half_sum_kernel(me_ref, *refs):
    count = len(refs) // 2
    for d in range(count):
        x = lax.rem(me_ref[0] + d, count)
        total = refs[0][x].astype(F32)
        for r in refs[1:count]:
            total = total + r[x].astype(F32)
        refs[count + d][...] = total.astype(BF16)


def half_sum(me, parts):
    vmem = pl.BlockSpec(memory_space=pltpu.VMEM)
    return pl.pallas_call(
        half_sum_kernel,
        in_specs=[pl.BlockSpec(memory_space=pltpu.SMEM)] + [vmem] * len(parts),
        out_shape=(jax.ShapeDtypeStruct(parts[0].shape[1:], BF16),) * len(parts),
        compiler_params=params(),
        name="half_sum",
    )(me, *parts)


def last_sum_kernel(out_ref, *refs):
    both_ref = refs[-1]
    width = out_ref.shape[2]
    total = out_ref[0].astype(F32)
    for s in range(1, out_ref.shape[0]):
        total = total + out_ref[s].astype(F32)
    both_ref[:, 0:width] = total.astype(BF16)
    total = refs[0][...].astype(F32)
    for r in refs[1:-1]:
        total = total + r[...].astype(F32)
    both_ref[:, width : 2 * width] = total.astype(BF16)


def last_sum(out_parts, grad_parts):
    _, total, width = out_parts.shape
    return pl.pallas_call(
        last_sum_kernel,
        out_shape=jax.ShapeDtypeStruct((total, 2 * width), BF16),
        compiler_params=params(),
        name="last_sum",
    )(out_parts, *grad_parts)


def combine_kernel(places_ref, weight_ref, back_ref, hid_ref, cot_ref, out_ref, grad_ref):
    block, width = hid_ref.shape
    slots = places_ref.shape[1]
    first = pl.program_id(0) * block
    where = lax.broadcasted_iota(jnp.int32, (block, slots), 0) + first
    picks = jnp.where(where == places_ref[...], 1.0, 0.0).astype(BF16)
    weighted = back_ref[:, 0:width].astype(F32) * weight_ref[...]
    high = weighted.astype(BF16)
    low = (weighted - high.astype(F32)).astype(BF16)
    terms = jnp.concatenate([high, low, back_ref[:, width : 2 * width]], axis=1)
    sums = jnp.dot(picks, terms, preferred_element_type=F32)
    combined = sums[:, 0:width] + sums[:, width : 2 * width]
    out_ref[...] = (hid_ref[...].astype(F32) + combined).astype(BF16)
    grad_ref[...] = (cot_ref[...].astype(F32) + sums[:, 2 * width : 3 * width]).astype(BF16)


def combine(places, weight, back, hidden, cotangent):
    length, width = hidden.shape
    slots = places.shape[1]
    block = 1024
    row_block = pl.BlockSpec((block, width), lambda i: (i, 0))

    def whole(shape):
        return pl.BlockSpec(shape, lambda i: (0, 0))

    return pl.pallas_call(
        combine_kernel,
        grid=(length // block,),
        in_specs=[
            whole((1, slots)),
            whole((slots, 1)),
            whole((slots, 2 * width)),
            row_block,
            row_block,
        ],
        out_specs=(row_block, row_block),
        out_shape=(jax.ShapeDtypeStruct(hidden.shape, BF16),) * 2,
        compiler_params=params(),
        name="combine",
    )(places, weight, back, hidden, cotangent)


def take_rows(array, index):
    return array.at[index].get(mode="promise_in_bounds")


def shift(block, dx, dy):
    side = SIDE
    moves = [
        (x * side + y, (x + dx) % side * side + (y + dy) % side)
        for x in range(side)
        for y in range(side)
    ]
    return lax.ppermute(block, "sp", moves)


def spread(block):
    copies = jnp.broadcast_to(block[None], (lax.axis_size("sp"),) + block.shape)
    return lax.all_to_all(copies, "sp", split_axis=0, concat_axis=0, tiled=True)


def on_device(
    queries,
    keys,
    values,
    residual,
    cotangent,
    gate_proj,
    up_proj,
    down_proj,
    chosen,
    counts,
    route_weight,
):
    rows = queries.shape[0]
    length, width = residual.shape
    places = chosen[0]
    experts = places.shape[0]
    slots = experts * SLOTS
    group = lax.axis_size("sp")
    side = SIDE
    x_groups = [[x * side + y for x in range(side)] for y in range(side)]
    y_groups = [[x * side + y for y in range(side)] for x in range(side)]
    x_me = (lax.axis_index("sp") // side).reshape(1)
    y_me = (lax.axis_index("sp") % side).reshape(1)

    packed = pack(queries, keys, values)
    qkv = lax.all_to_all(packed, "sp", split_axis=0, concat_axis=0, tiled=True)

    live = jnp.arange(SLOTS, dtype=jnp.int32)[None, :] < counts[0][:, None]
    weight = jnp.where(live, route_weight[0], jnp.float32(0.0)).reshape(slots, 1)
    flat = places.reshape(slots)
    picked_residual = take_rows(residual, flat)
    tangent = (take_rows(cotangent, flat).astype(F32) * weight).astype(BF16)
    all_tangents = lax.all_gather(tangent.reshape(experts, SLOTS, width), "ep", axis=0)
    own_tangents = lax.dynamic_index_in_dim(all_tangents, lax.axis_index("ep"), 1, False)
    owned_tangent = lax.all_gather(own_tangents.reshape(-1, width), "sp", axis=0)

    query_rows = (flat // rows) * (3 * rows) + flat % rows
    picked_queries = take_rows(qkv.reshape(-1, HD), query_rows)
    block = min(512, slots)
    picked_hidden = attention(
        picked_queries,
        pl.BlockSpec((block, HD), lambda i: (i, 0)),
        picked_residual,
        0,
        slots,
        qkv,
        block,
        "picked_attention",
    )

    def full_attention(first, count, queries_here):
        return attention(
            queries_here,
            pl.BlockSpec((2, rows, HD), lambda i: (i + first, 0, 0)),
            residual,
            first,
            count * 2 * rows,
            qkv,
            2 * rows,
            "full_attention",
        )

    owned = lax.all_to_all(
        picked_hidden.reshape(experts, SLOTS, width), "ep", split_axis=0, concat_axis=0, tiled=True
    ).reshape(-1, width)
    half = group // 4
    owned, queries_now = lax.optimization_barrier((owned, qkv))
    owned_rows = spread(owned)
    hidden_first = full_attention(0, half, queries_now)
    gate, up, down = gate_proj[0], up_proj[0], down_proj[0]
    d_act = tangent_product(owned_tangent, down)
    owned_rows, d_act, hidden_first = lax.optimization_barrier((owned_rows, d_act, hidden_first))
    act, out_part, *grad_parts = expert(y_me, owned_rows, d_act, gate, up, down, side)

    act, out_part, queries_now = lax.optimization_barrier((act, out_part, qkv))
    out_part = lax.all_to_all(
        out_part.reshape(side, -1, width),
        "sp",
        split_axis=0,
        concat_axis=0,
        axis_index_groups=x_groups,
        tiled=True,
    )
    grad_parts = [grad_parts[0]] + [shift(grad_parts[d], 0, d) for d in range(1, side)]
    grad_down = down_grad(act, owned_tangent)
    hidden_second = full_attention(half, half, queries_now)
    out_part, grad_down, hidden_second = lax.optimization_barrier(
        (out_part, grad_down, hidden_second)
    )
    out_part = jnp.sum(out_part.astype(F32).reshape(side, side, -1, width), axis=0).astype(BF16)
    out_part = lax.all_to_all(
        out_part, "sp", split_axis=0, concat_axis=0, axis_index_groups=y_groups, tiled=True
    )
    grad_parts = half_sum(x_me, grad_parts)
    grad_parts = [grad_parts[0]] + [shift(grad_parts[d], d, 0) for d in range(1, side)]
    back = last_sum(out_part, grad_parts).reshape(-1, SLOTS, 2 * width)
    back = lax.all_to_all(back, "ep", split_axis=0, concat_axis=0, tiled=True)
    block_out, grad_hidden = combine(
        flat.reshape(1, slots),
        weight,
        back.reshape(slots, 2 * width),
        jnp.concatenate([hidden_first, hidden_second], axis=0),
        cotangent,
    )
    return (block_out, grad_hidden, grad_down[None])


def solution(mesh):
    in_specs = (
        P(("ep", "sp"), None),
        P(("ep", "sp"), None),
        P(("ep", "sp"), None),
        P("ep", "sp"),
        P("ep", "sp"),
        P("ep", None, "sp"),
        P("ep", None, "sp"),
        P("ep", "sp", None),
        P("ep", None, None),
        P("ep", None),
        P("ep", None, None),
    )
    out_specs = (P("ep", "sp"), P("ep", "sp"), P("ep", "sp", None))
    return jax.shard_map(
        on_device, mesh=mesh, in_specs=in_specs, out_specs=out_specs, check_vma=False
    )
```

```python
import functools

import jax
import jax.numpy as jnp
from jax import lax
from jax.experimental import pallas as pl
from jax.experimental.pallas import tpu as pltpu
from jax.sharding import PartitionSpec as P

HD = 128
SLOTS = 32
SIDE = 4
LOG2E = 1.4426950408889634
VMEM_LIMIT = 48 * 1024 * 1024
BIG_VMEM = 60 * 1024 * 1024
SAFE_EXPONENT = 110.0
F32 = jnp.float32
BF16 = jnp.bfloat16
OVER_LAST = (((1,), (1,)), ((), ()))


def params(limit=VMEM_LIMIT):
    return pltpu.CompilerParams(vmem_limit_bytes=limit)


def pack_kernel(q_hbm, k_hbm, v_hbm, out_hbm, stage_ref, in_sems, out_sems):
    rows, width = q_hbm.shape
    heads = width // HD
    sources = (q_hbm, k_hbm, v_hbm)
    loads = []
    for h in range(heads):
        for i, ref in enumerate(sources):
            loads.append(
                pltpu.make_async_copy(
                    ref.at[:, pl.ds(h * HD, HD)],
                    stage_ref.at[h, pl.ds(i * rows, rows), :],
                    in_sems.at[3 * h + i],
                )
            )
    for copy in loads:
        copy.start()
    stores = [
        pltpu.make_async_copy(stage_ref.at[h], out_hbm.at[h], out_sems.at[h]) for h in range(heads)
    ]
    for h in range(heads):
        for copy in loads[3 * h : 3 * h + 3]:
            copy.wait()
        stores[h].start()
    for copy in stores:
        copy.wait()


def pack(queries, keys, values):
    rows, width = queries.shape
    heads = width // HD
    shape = (heads, 3 * rows, HD)
    hbm = pl.BlockSpec(memory_space=pltpu.HBM)
    return pl.pallas_call(
        pack_kernel,
        in_specs=[hbm] * 3,
        out_specs=hbm,
        out_shape=jax.ShapeDtypeStruct(shape, BF16),
        scratch_shapes=[
            pltpu.VMEM(shape, BF16),
            pltpu.SemaphoreType.DMA((3 * heads,)),
            pltpu.SemaphoreType.DMA((heads,)),
        ],
        compiler_params=params(BIG_VMEM),
        name="pack_qkv",
    )(queries, keys, values)


def attention_kernel(rows, q_ref, res_ref, qkv_ref, out_ref, peak_ref):
    sources = qkv_ref.shape[0]
    block = res_ref.shape[0]
    part = min(256, block)
    scale = HD**-0.5 * LOG2E

    @pl.when(pl.program_id(0) == 0)
    def _():
        peak = jnp.zeros((rows, HD), F32)
        for s in range(sources):
            key = qkv_ref[s, rows : 2 * rows, :].astype(F32)
            square = (key * key).astype(BF16)
            peak = jnp.maximum(
                peak, jnp.dot(square, jnp.ones((HD, HD), BF16), preferred_element_type=F32)
            )
        peak_ref[0] = jnp.max(peak)

    query = q_ref[...].reshape(block, HD)
    wide_query = query.astype(F32)
    longest = jnp.max(jnp.sum(wide_query * wide_query, axis=1, keepdims=True))
    small = longest * peak_ref[0] * (1.02 * scale * scale) <= SAFE_EXPONENT * SAFE_EXPONENT

    def scores_of(here, s):
        return (
            lax.dot_general(
                query[here], qkv_ref[s, rows : 2 * rows, :], OVER_LAST, preferred_element_type=F32
            )
            * scale
        )

    def finish(here, total, norm):
        norm = jnp.sum(norm, axis=1, keepdims=True)
        attended = (total / norm).astype(BF16)
        out_ref[here, :] = (res_ref[here, :].astype(F32) + attended.astype(F32)).astype(BF16)

    def add_up(here, shift):
        total = jnp.zeros((part, HD), F32)
        norm = jnp.zeros((part, HD), F32)
        for s in range(sources):
            scores = scores_of(here, s)
            probs = jnp.exp2(scores if shift is None else scores - shift)
            for c in range(rows // HD):
                norm = norm + probs[:, c * HD : (c + 1) * HD]
            total = total + jnp.dot(
                probs.astype(BF16), qkv_ref[s, 2 * rows : 3 * rows, :], preferred_element_type=F32
            )
        finish(here, total, norm)

    @pl.when(small)
    def _():
        for p in range(block // part):
            add_up(slice(p * part, (p + 1) * part), None)

    @pl.when(jnp.logical_not(small))
    def _():
        for p in range(block // part):
            here = slice(p * part, (p + 1) * part)
            top = jnp.full((part, 1), -jnp.inf, F32)
            for s in range(sources):
                top = jnp.maximum(top, jnp.max(scores_of(here, s), axis=1, keepdims=True))
            add_up(here, top)


def attention(queries, query_spec, residual, residual_first, total, qkv, block, name):
    sources, rows3, _ = qkv.shape
    rows = rows3 // 3
    length = sources * rows
    return pl.pallas_call(
        functools.partial(attention_kernel, rows),
        grid=(total // block,),
        in_specs=[
            query_spec,
            pl.BlockSpec((block, HD), lambda i: (i + residual_first, 0)),
            pl.BlockSpec((sources, rows3, HD), lambda i: (0, 0, 0)),
        ],
        out_specs=pl.BlockSpec((block, HD), lambda i: (i, 0)),
        out_shape=jax.ShapeDtypeStruct((total, HD), BF16),
        scratch_shapes=[pltpu.SMEM((1,), F32)],
        compiler_params=params(),
        cost_estimate=pl.CostEstimate(
            flops=8 * total * length * HD,
            bytes_accessed=4 * total * HD * 2 + qkv.size * 2,
            transcendentals=total * length,
        ),
        name=name,
    )(queries, residual, qkv)


def wide_rows(ref):
    return jnp.concatenate([ref[c] for c in range(ref.shape[0])], axis=1)


def tangent_kernel(tan_ref, down_ref, d_act_ref):
    d_act_ref[...] = lax.dot_general(
        wide_rows(tan_ref), down_ref[...], OVER_LAST, preferred_element_type=F32
    )


def tangent_product(tangent, down):
    blocks, total, width = tangent.shape
    hidden = down.shape[0]
    return pl.pallas_call(
        tangent_kernel,
        out_shape=jax.ShapeDtypeStruct((total, hidden), F32),
        compiler_params=params(),
        cost_estimate=pl.CostEstimate(
            flops=2 * total * hidden * blocks * width,
            bytes_accessed=2 * tangent.size + 2 * down.size + 4 * total * hidden,
            transcendentals=0,
        ),
        name="tangent_product",
    )(tangent, down)


def in_pieces(src, dst, sems, first, pieces=4):
    rows = src.shape[0] // pieces
    return [
        pltpu.make_async_copy(
            src.at[pl.ds(i * rows, rows)], dst.at[pl.ds(i * rows, rows)], sems.at[first + i]
        )
        for i in range(pieces)
    ]


def expert_kernel(
    me_ref, x_hbm, d_act_hbm, gate_hbm, up_hbm, down_hbm, act_hbm, out_hbm, *rest
):
    *grad_hbm, x_ref, d_act_ref, gate_ref, up_ref, down_ref, act_ref = rest[:-4]
    out_ref, stage_ref, in_sems, out_sems = rest[-4:]
    side, _, _, _, width = x_hbm.shape
    blocks = side * side
    load_x = [
        pltpu.make_async_copy(
            x_hbm.at[c // side, :, c % side],
            x_ref.at[:, :, pl.ds(c * width, width)],
            in_sems.at[12 + c],
        )
        for c in range(blocks)
    ]
    load_gate = in_pieces(gate_hbm, gate_ref, in_sems, 0)
    load_up = in_pieces(up_hbm, up_ref, in_sems, 4)
    load_d_act = in_pieces(d_act_hbm, d_act_ref, in_sems, 8)
    load_down = in_pieces(down_hbm, down_ref, in_sems, 12 + blocks)
    for copy in load_gate + load_x + load_up + load_down + load_d_act:
        copy.start()
    for copy in load_gate + load_x:
        copy.wait()
    rows = x_ref[...].reshape(act_ref.shape[0], blocks * width)
    gate_pre = jnp.dot(rows, gate_ref[...], preferred_element_type=F32)
    for copy in load_up:
        copy.wait()
    up_pre = jnp.dot(rows, up_ref[...], preferred_element_type=F32)
    sig = jax.nn.sigmoid(gate_pre)
    silu = gate_pre * sig
    act = (silu * up_pre).astype(BF16)
    act_ref[...] = act
    stores = in_pieces(act_ref, act_hbm, out_sems, 4 * side)
    for copy in stores:
        copy.start()
    for copy in load_down:
        copy.wait()
    for c in range(0, blocks, 2):
        pair = jnp.dot(
            act, down_ref[:, c * width : (c + 2) * width], preferred_element_type=F32
        ).astype(BF16)
        out_ref[c] = pair[:, 0:width]
        out_ref[c + 1] = pair[:, width : 2 * width]
        here = pl.ds(c, 2)
        stores.append(
            pltpu.make_async_copy(
                out_ref.at[here], out_hbm.at[here], out_sems.at[4 * side + 4 + c // 2]
            )
        )
        stores[-1].start()
    for copy in load_d_act:
        copy.wait()
    d_act = d_act_ref[...]
    d_gate = (d_act * up_pre * sig * (1.0 + gate_pre * (1.0 - sig))).astype(BF16)
    d_up = (d_act * silu).astype(BF16)
    for d in list(range(1, side)) + [0]:
        y = lax.rem(me_ref[0] + d, side)
        for x in range(0, side, 2):
            first = pl.ds(pl.multiple_of((x * side + y) * width, width), width)
            second = pl.ds(pl.multiple_of(((x + 1) * side + y) * width, width), width)
            gate = jnp.concatenate([gate_ref[first, :], gate_ref[second, :]], axis=0)
            up = jnp.concatenate([up_ref[first, :], up_ref[second, :]], axis=0)
            pair = lax.dot_general(d_gate, gate, OVER_LAST, preferred_element_type=F32)
            pair = pair + lax.dot_general(d_up, up, OVER_LAST, preferred_element_type=F32)
            pair = pair.astype(BF16)
            stage_ref[d, x] = pair[:, 0:width]
            stage_ref[d, x + 1] = pair[:, width : 2 * width]
        here = in_pieces(stage_ref.at[d], grad_hbm[d], out_sems, 4 * d)
        for copy in here:
            copy.start()
        stores += here
    for copy in stores:
        copy.wait()


def expert(me, rows, d_act, gate, up, down):
    side, images, _, slots, width = rows.shape
    blocks = side * side
    total = images * slots
    hidden = gate.shape[1]
    quarter = jax.ShapeDtypeStruct((blocks // side, total, width), BF16)
    hbm = pl.BlockSpec(memory_space=pltpu.HBM)
    return pl.pallas_call(
        expert_kernel,
        in_specs=[pl.BlockSpec(memory_space=pltpu.SMEM)] + [hbm] * 5,
        out_specs=(hbm,) * (side + 2),
        out_shape=(
            jax.ShapeDtypeStruct((total, hidden), BF16),
            jax.ShapeDtypeStruct((blocks, total, width), BF16),
        )
        + (quarter,) * side,
        scratch_shapes=[
            pltpu.VMEM((images, slots, blocks * width), BF16),
            pltpu.VMEM(d_act.shape, F32),
            pltpu.VMEM(gate.shape, BF16),
            pltpu.VMEM(up.shape, BF16),
            pltpu.VMEM(down.shape, BF16),
            pltpu.VMEM((total, hidden), BF16),
            pltpu.VMEM((blocks, total, width), BF16),
            pltpu.VMEM((side,) + quarter.shape, BF16),
            pltpu.SemaphoreType.DMA((16 + blocks,)),
            pltpu.SemaphoreType.DMA((4 * side + 4 + blocks // 2,)),
        ],
        compiler_params=params(BIG_VMEM),
        cost_estimate=pl.CostEstimate(
            flops=10 * total * hidden * blocks * width,
            bytes_accessed=4 * rows.size + 4 * gate.size + 6 * total * hidden,
            transcendentals=total * hidden,
        ),
        name="expert",
    )(me, rows, d_act, gate, up, down)


def down_grad_kernel(act_ref, tan_ref, grad_ref):
    tangent = wide_rows(tan_ref)
    grad_ref[...] = lax.dot_general(
        act_ref[...], tangent, (((0,), (0,)), ((), ())), preferred_element_type=F32
    ).astype(BF16)


def down_grad(act, tangent):
    blocks, total, width = tangent.shape
    hidden = act.shape[1]
    return pl.pallas_call(
        down_grad_kernel,
        out_shape=jax.ShapeDtypeStruct((hidden, blocks * width), BF16),
        compiler_params=params(),
        cost_estimate=pl.CostEstimate(
            flops=2 * total * hidden * blocks * width,
            bytes_accessed=2 * tangent.size + 2 * total * hidden + 2 * hidden * blocks * width,
            transcendentals=0,
        ),
        name="down_grad",
    )(act, tangent)


def quarter_sum_kernel(in_ref, out_ref):
    for b in range(out_ref.shape[0]):
        total = in_ref[0, b].astype(F32)
        for s in range(1, in_ref.shape[0]):
            total = total + in_ref[s, b].astype(F32)
        out_ref[b] = total.astype(BF16)


def quarter_sum(parts):
    return pl.pallas_call(
        quarter_sum_kernel,
        out_shape=jax.ShapeDtypeStruct(parts.shape[1:], BF16),
        compiler_params=params(),
        name="quarter_sum",
    )(parts)


def half_sum_kernel(me_ref, *refs):
    count = len(refs) // 2
    for d in range(count):
        x = lax.rem(me_ref[0] + d, count)
        total = refs[0][x].astype(F32)
        for r in refs[1:count]:
            total = total + r[x].astype(F32)
        refs[count + d][...] = total.astype(BF16)


def half_sum(me, parts):
    vmem = pl.BlockSpec(memory_space=pltpu.VMEM)
    return pl.pallas_call(
        half_sum_kernel,
        in_specs=[pl.BlockSpec(memory_space=pltpu.SMEM)] + [vmem] * len(parts),
        out_shape=(jax.ShapeDtypeStruct(parts[0].shape[1:], BF16),) * len(parts),
        compiler_params=params(),
        name="half_sum",
    )(me, *parts)


def last_sum_kernel(out_ref, *refs):
    both_ref = refs[-1]
    width = out_ref.shape[2]
    total = out_ref[0].astype(F32)
    for s in range(1, out_ref.shape[0]):
        total = total + out_ref[s].astype(F32)
    both_ref[:, 0:width] = total.astype(BF16)
    total = refs[0][...].astype(F32)
    for r in refs[1:-1]:
        total = total + r[...].astype(F32)
    both_ref[:, width : 2 * width] = total.astype(BF16)


def last_sum(out_parts, grad_parts):
    _, total, width = out_parts.shape
    return pl.pallas_call(
        last_sum_kernel,
        out_shape=jax.ShapeDtypeStruct((total, 2 * width), BF16),
        compiler_params=params(),
        name="last_sum",
    )(out_parts, *grad_parts)


def combine_kernel(places_ref, weight_ref, back_ref, hid_ref, cot_ref, out_ref, grad_ref):
    block, width = hid_ref.shape
    slots = places_ref.shape[1]
    first = pl.program_id(0) * block
    where = lax.broadcasted_iota(jnp.int32, (block, slots), 0) + first
    picks = jnp.where(where == places_ref[...], 1.0, 0.0).astype(BF16)
    weighted = back_ref[:, 0:width].astype(F32) * weight_ref[...]
    terms = jnp.concatenate([weighted.astype(BF16), back_ref[:, width : 2 * width]], axis=1)
    sums = jnp.dot(picks, terms, preferred_element_type=F32)
    out_ref[...] = (hid_ref[...].astype(F32) + sums[:, 0:width]).astype(BF16)
    grad_ref[...] = (cot_ref[...].astype(F32) + sums[:, width : 2 * width]).astype(BF16)


def combine(places, weight, back, hidden, cotangent):
    length, width = hidden.shape
    slots = places.shape[1]
    block = 1024
    row_block = pl.BlockSpec((block, width), lambda i: (i, 0))

    def whole(shape):
        return pl.BlockSpec(shape, lambda i: (0, 0))

    return pl.pallas_call(
        combine_kernel,
        grid=(length // block,),
        in_specs=[
            whole((1, slots)),
            whole((slots, 1)),
            whole((slots, 2 * width)),
            row_block,
            row_block,
        ],
        out_specs=(row_block, row_block),
        out_shape=(jax.ShapeDtypeStruct(hidden.shape, BF16),) * 2,
        compiler_params=params(),
        name="combine",
    )(places, weight, back, hidden, cotangent)


def take_rows(array, index):
    return array.at[index].get(mode="promise_in_bounds")


def shift(block, dx, dy):
    side = SIDE
    moves = [
        (x * side + y, (x + dx) % side * side + (y + dy) % side)
        for x in range(side)
        for y in range(side)
    ]
    return lax.ppermute(block, "sp", moves)


def on_device(
    queries,
    keys,
    values,
    residual,
    cotangent,
    gate_proj,
    up_proj,
    down_proj,
    chosen,
    counts,
    route_weight,
):
    rows = queries.shape[0]
    length, width = residual.shape
    places = chosen[0]
    experts = places.shape[0]
    slots = experts * SLOTS
    group = lax.axis_size("sp")
    side = SIDE
    x_groups = [[x * side + y for x in range(side)] for y in range(side)]
    y_groups = [[x * side + y for y in range(side)] for x in range(side)]
    x_me = (lax.axis_index("sp") // side).reshape(1)
    y_me = (lax.axis_index("sp") % side).reshape(1)

    packed = pack(queries, keys, values)
    packed, cotangent_now, residual_now, flat, counts, route_weight = lax.optimization_barrier(
        (packed, cotangent, residual, places.reshape(slots), counts, route_weight)
    )
    qkv = lax.all_to_all(packed, "sp", split_axis=0, concat_axis=0, tiled=True)

    live = jnp.arange(SLOTS, dtype=jnp.int32)[None, :] < counts[0][:, None]
    weight = jnp.where(live, route_weight[0], jnp.float32(0.0)).reshape(slots, 1)
    picked_residual = take_rows(residual_now, flat)
    tangent = (take_rows(cotangent_now, flat).astype(F32) * weight).astype(BF16)
    all_tangents = lax.all_gather(tangent.reshape(experts, SLOTS, width), "ep", axis=0)
    own_tangents = lax.dynamic_index_in_dim(all_tangents, lax.axis_index("ep"), 1, False)
    own_tangents = own_tangents.reshape(-1, width)
    qkv, picked_residual = lax.optimization_barrier((qkv, picked_residual))
    owned_tangent = lax.all_gather(own_tangents, "sp", axis=0)

    query_rows = (flat // rows) * (3 * rows) + flat % rows
    picked_queries = take_rows(qkv.reshape(-1, HD), query_rows)
    block = min(512, slots)
    picked_hidden = attention(
        picked_queries,
        pl.BlockSpec((block, HD), lambda i: (i, 0)),
        picked_residual,
        0,
        slots,
        qkv,
        block,
        "picked_attention",
    )
    def full_attention(first, count, queries_here):
        return attention(
            queries_here,
            pl.BlockSpec((2, rows, HD), lambda i: (i + first, 0, 0)),
            residual,
            first,
            count * 2 * rows,
            qkv,
            2 * rows,
            "full_attention",
        )

    to_rows = jnp.broadcast_to(
        picked_hidden.reshape(experts, 1, SLOTS, width), (experts, side, SLOTS, width)
    )
    owned = lax.all_to_all(
        to_rows.reshape(-1, SLOTS, width),
        ("ep", "sp"),
        split_axis=0,
        concat_axis=0,
        axis_index_groups=[
            [e * group + x * side + y for e in range(experts) for y in range(side)]
            for x in range(side)
        ],
        tiled=True,
    )
    half = group // 4
    owned, queries_now = lax.optimization_barrier((owned, qkv))
    copies = jnp.broadcast_to(owned[None], (side,) + owned.shape)
    owned_rows = lax.all_to_all(
        copies.reshape(side, -1, width),
        "sp",
        split_axis=0,
        concat_axis=0,
        axis_index_groups=x_groups,
        tiled=True,
    ).reshape(side, experts, side, SLOTS, width)
    hidden_first = full_attention(0, half, queries_now)
    gate, up, down = gate_proj[0], up_proj[0], down_proj[0]
    d_act = tangent_product(owned_tangent, down)
    owned_rows, d_act, hidden_first = lax.optimization_barrier((owned_rows, d_act, hidden_first))
    act, out_part, *grad_parts = expert(y_me, owned_rows, d_act, gate, up, down)

    act, out_part, queries_now = lax.optimization_barrier((act, out_part, qkv))
    out_part = lax.all_to_all(
        out_part.reshape(side, -1, width),
        "sp",
        split_axis=0,
        concat_axis=0,
        axis_index_groups=x_groups,
        tiled=True,
    )
    grad_parts = [grad_parts[0]] + [shift(grad_parts[d], 0, d) for d in range(1, side)]
    grad_down = down_grad(act, owned_tangent)
    hidden_second = full_attention(half, half, queries_now)
    out_part, grad_down, hidden_second = lax.optimization_barrier(
        (out_part, grad_down, hidden_second)
    )
    out_part = quarter_sum(out_part.reshape(side, side, -1, width))
    out_part = lax.all_to_all(
        out_part, "sp", split_axis=0, concat_axis=0, axis_index_groups=y_groups, tiled=True
    )
    grad_parts = half_sum(x_me, grad_parts)
    grad_parts = [grad_parts[0]] + [shift(grad_parts[d], d, 0) for d in range(1, side)]
    back = last_sum(out_part, grad_parts).reshape(-1, SLOTS, 2 * width)
    back = lax.all_to_all(back, "ep", split_axis=0, concat_axis=0, tiled=True)
    block_out, grad_hidden = combine(
        flat.reshape(1, slots),
        weight,
        back.reshape(slots, 2 * width),
        jnp.concatenate([hidden_first, hidden_second], axis=0),
        cotangent,
    )
    return (block_out, grad_hidden, grad_down[None])


def solution(mesh):
    in_specs = (
        P(("ep", "sp"), None),
        P(("ep", "sp"), None),
        P(("ep", "sp"), None),
        P("ep", "sp"),
        P("ep", "sp"),
        P("ep", None, "sp"),
        P("ep", None, "sp"),
        P("ep", "sp", None),
        P("ep", None, None),
        P("ep", None),
        P("ep", None, None),
    )
    out_specs = (P("ep", "sp"), P("ep", "sp"), P("ep", "sp", None))
    return jax.shard_map(
        on_device, mesh=mesh, in_specs=in_specs, out_specs=out_specs, check_vma=False
    )
```

```python
import functools

import jax
import jax.numpy as jnp
from jax import lax
from jax.experimental import pallas as pl
from jax.experimental.pallas import tpu as pltpu
from jax.sharding import PartitionSpec as P

HD = 128
SLOTS = 32
SIDE = 4
LOG2E = 1.4426950408889634
VMEM_LIMIT = 48 * 1024 * 1024
BIG_VMEM = 60 * 1024 * 1024
SAFE_EXPONENT = 110.0
F32 = jnp.float32
BF16 = jnp.bfloat16
OVER_LAST = (((1,), (1,)), ((), ()))


def params(limit=VMEM_LIMIT):
    return pltpu.CompilerParams(vmem_limit_bytes=limit)


def in_pieces(src, dst, sems, first, pieces=4):
    rows = src.shape[0] // pieces
    return [
        pltpu.make_async_copy(
            src.at[pl.ds(i * rows, rows)], dst.at[pl.ds(i * rows, rows)], sems.at[first + i]
        )
        for i in range(pieces)
    ]


def pack_kernel(q_hbm, k_hbm, v_hbm, out_hbm, q_ref, k_ref, v_ref, in_sems, out_sems):
    rows, width = q_hbm.shape
    heads = width // HD
    refs = (q_ref, k_ref, v_ref)
    loads = [
        in_pieces(src, dst, in_sems, 4 * i)
        for i, (src, dst) in enumerate(zip((q_hbm, k_hbm, v_hbm), refs))
    ]
    for pieces in loads:
        for copy in pieces:
            copy.start()
    stores = []
    for i, ref in enumerate(refs):
        for copy in loads[i]:
            copy.wait()
        for h in range(heads):
            stores.append(
                pltpu.make_async_copy(
                    ref.at[:, pl.ds(h * HD, HD)],
                    out_hbm.at[h, pl.ds(i * rows, rows), :],
                    out_sems.at[heads * i + h],
                )
            )
            stores[-1].start()
    for copy in stores:
        copy.wait()


def pack(queries, keys, values):
    rows, width = queries.shape
    heads = width // HD
    hbm = pl.BlockSpec(memory_space=pltpu.HBM)
    return pl.pallas_call(
        pack_kernel,
        in_specs=[hbm] * 3,
        out_specs=hbm,
        out_shape=jax.ShapeDtypeStruct((heads, 3 * rows, HD), BF16),
        scratch_shapes=[pltpu.VMEM(queries.shape, BF16)] * 3
        + [pltpu.SemaphoreType.DMA((12,)), pltpu.SemaphoreType.DMA((3 * heads,))],
        compiler_params=params(BIG_VMEM),
        name="pack_qkv",
    )(queries, keys, values)


def attention_kernel(rows, q_ref, res_ref, qkv_ref, out_ref, peak_ref):
    sources = qkv_ref.shape[0]
    block = res_ref.shape[0]
    part = min(256, block)
    scale = HD**-0.5 * LOG2E

    @pl.when(pl.program_id(0) == 0)
    def _():
        peak = jnp.zeros((rows, HD), F32)
        for s in range(sources):
            key = qkv_ref[s, rows : 2 * rows, :].astype(F32)
            square = (key * key).astype(BF16)
            peak = jnp.maximum(
                peak, jnp.dot(square, jnp.ones((HD, HD), BF16), preferred_element_type=F32)
            )
        peak_ref[0] = jnp.max(peak)

    query = q_ref[...].reshape(block, HD)
    wide_query = query.astype(F32)
    longest = jnp.max(jnp.sum(wide_query * wide_query, axis=1, keepdims=True))
    small = longest * peak_ref[0] * (1.02 * scale * scale) <= SAFE_EXPONENT * SAFE_EXPONENT

    def scores_of(here, s):
        return (
            lax.dot_general(
                query[here], qkv_ref[s, rows : 2 * rows, :], OVER_LAST, preferred_element_type=F32
            )
            * scale
        )

    def finish(here, total, norm):
        norm = jnp.sum(norm, axis=1, keepdims=True)
        attended = (total / norm).astype(BF16)
        out_ref[here, :] = (res_ref[here, :].astype(F32) + attended.astype(F32)).astype(BF16)

    def add_up(here, shift):
        total = jnp.zeros((part, HD), F32)
        norm = jnp.zeros((part, HD), F32)
        for s in range(sources):
            scores = scores_of(here, s)
            probs = jnp.exp2(scores if shift is None else scores - shift)
            for c in range(rows // HD):
                norm = norm + probs[:, c * HD : (c + 1) * HD]
            total = total + jnp.dot(
                probs.astype(BF16), qkv_ref[s, 2 * rows : 3 * rows, :], preferred_element_type=F32
            )
        finish(here, total, norm)

    @pl.when(small)
    def _():
        for p in range(block // part):
            add_up(slice(p * part, (p + 1) * part), None)

    @pl.when(jnp.logical_not(small))
    def _():
        for p in range(block // part):
            here = slice(p * part, (p + 1) * part)
            top = jnp.full((part, 1), -jnp.inf, F32)
            for s in range(sources):
                top = jnp.maximum(top, jnp.max(scores_of(here, s), axis=1, keepdims=True))
            add_up(here, top)


def attention(queries, query_spec, residual, residual_first, total, qkv, block, name):
    sources, rows3, _ = qkv.shape
    rows = rows3 // 3
    length = sources * rows
    return pl.pallas_call(
        functools.partial(attention_kernel, rows),
        grid=(total // block,),
        in_specs=[
            query_spec,
            pl.BlockSpec((block, HD), lambda i: (i + residual_first, 0)),
            pl.BlockSpec((sources, rows3, HD), lambda i: (0, 0, 0)),
        ],
        out_specs=pl.BlockSpec((block, HD), lambda i: (i, 0)),
        out_shape=jax.ShapeDtypeStruct((total, HD), BF16),
        scratch_shapes=[pltpu.SMEM((1,), F32)],
        compiler_params=params(),
        cost_estimate=pl.CostEstimate(
            flops=8 * total * length * HD,
            bytes_accessed=4 * total * HD * 2 + qkv.size * 2,
            transcendentals=total * length,
        ),
        name=name,
    )(queries, residual, qkv)


def wide_rows(ref):
    return jnp.concatenate([ref[c] for c in range(ref.shape[0])], axis=1)


def tangent_kernel(tan_ref, down_ref, d_act_ref):
    d_act_ref[...] = lax.dot_general(
        wide_rows(tan_ref), down_ref[...], OVER_LAST, preferred_element_type=F32
    )


def tangent_product(tangent, down):
    blocks, total, width = tangent.shape
    hidden = down.shape[0]
    return pl.pallas_call(
        tangent_kernel,
        out_shape=jax.ShapeDtypeStruct((total, hidden), F32),
        compiler_params=params(),
        cost_estimate=pl.CostEstimate(
            flops=2 * total * hidden * blocks * width,
            bytes_accessed=2 * tangent.size + 2 * down.size + 4 * total * hidden,
            transcendentals=0,
        ),
        name="tangent_product",
    )(tangent, down)


def expert_kernel(
    me_ref, x_hbm, d_act_hbm, gate_hbm, up_hbm, down_hbm, act_hbm, out_hbm, *rest
):
    *grad_hbm, x_ref, d_act_ref, gate_ref, up_ref, down_ref, act_ref = rest[:-4]
    out_ref, stage_ref, in_sems, out_sems = rest[-4:]
    side, _, _, _, width = x_hbm.shape
    blocks = side * side
    load_x = [
        pltpu.make_async_copy(
            x_hbm.at[c // side, :, c % side],
            x_ref.at[:, :, pl.ds(c * width, width)],
            in_sems.at[12 + c],
        )
        for c in range(blocks)
    ]
    load_gate = in_pieces(gate_hbm, gate_ref, in_sems, 0)
    load_up = in_pieces(up_hbm, up_ref, in_sems, 4)
    load_d_act = in_pieces(d_act_hbm, d_act_ref, in_sems, 8)
    load_down = in_pieces(down_hbm, down_ref, in_sems, 12 + blocks)
    for copy in load_gate + load_x + load_up + load_down + load_d_act:
        copy.start()
    for copy in load_gate + load_x:
        copy.wait()
    rows = x_ref[...].reshape(act_ref.shape[0], blocks * width)
    gate_pre = jnp.dot(rows, gate_ref[...], preferred_element_type=F32)
    for copy in load_up:
        copy.wait()
    up_pre = jnp.dot(rows, up_ref[...], preferred_element_type=F32)
    sig = jax.nn.sigmoid(gate_pre)
    silu = gate_pre * sig
    act = (silu * up_pre).astype(BF16)
    act_ref[...] = act
    stores = in_pieces(act_ref, act_hbm, out_sems, 4 * side)
    for copy in stores:
        copy.start()
    for copy in load_down:
        copy.wait()
    for c in range(0, blocks, 2):
        pair = jnp.dot(
            act, down_ref[:, c * width : (c + 2) * width], preferred_element_type=F32
        ).astype(BF16)
        out_ref[c] = pair[:, 0:width]
        out_ref[c + 1] = pair[:, width : 2 * width]
        here = pl.ds(c, 2)
        stores.append(
            pltpu.make_async_copy(
                out_ref.at[here], out_hbm.at[here], out_sems.at[4 * side + 4 + c // 2]
            )
        )
        stores[-1].start()
    for copy in load_d_act:
        copy.wait()
    d_act = d_act_ref[...]
    d_gate = (d_act * up_pre * sig * (1.0 + gate_pre * (1.0 - sig))).astype(BF16)
    d_up = (d_act * silu).astype(BF16)
    for d in list(range(1, side)) + [0]:
        y = lax.rem(me_ref[0] + d, side)
        for x in range(0, side, 2):
            first = pl.ds(pl.multiple_of((x * side + y) * width, width), width)
            second = pl.ds(pl.multiple_of(((x + 1) * side + y) * width, width), width)
            gate = jnp.concatenate([gate_ref[first, :], gate_ref[second, :]], axis=0)
            up = jnp.concatenate([up_ref[first, :], up_ref[second, :]], axis=0)
            pair = lax.dot_general(d_gate, gate, OVER_LAST, preferred_element_type=F32)
            pair = pair + lax.dot_general(d_up, up, OVER_LAST, preferred_element_type=F32)
            pair = pair.astype(BF16)
            stage_ref[d, x] = pair[:, 0:width]
            stage_ref[d, x + 1] = pair[:, width : 2 * width]
        here = in_pieces(stage_ref.at[d], grad_hbm[d], out_sems, 4 * d)
        for copy in here:
            copy.start()
        stores += here
    for copy in stores:
        copy.wait()


def expert(me, rows, d_act, gate, up, down):
    side, images, _, slots, width = rows.shape
    blocks = side * side
    total = images * slots
    hidden = gate.shape[1]
    quarter = jax.ShapeDtypeStruct((blocks // side, total, width), BF16)
    hbm = pl.BlockSpec(memory_space=pltpu.HBM)
    return pl.pallas_call(
        expert_kernel,
        in_specs=[pl.BlockSpec(memory_space=pltpu.SMEM)] + [hbm] * 5,
        out_specs=(hbm,) * (side + 2),
        out_shape=(
            jax.ShapeDtypeStruct((total, hidden), BF16),
            jax.ShapeDtypeStruct((blocks, total, width), BF16),
        )
        + (quarter,) * side,
        scratch_shapes=[
            pltpu.VMEM((images, slots, blocks * width), BF16),
            pltpu.VMEM(d_act.shape, F32),
            pltpu.VMEM(gate.shape, BF16),
            pltpu.VMEM(up.shape, BF16),
            pltpu.VMEM(down.shape, BF16),
            pltpu.VMEM((total, hidden), BF16),
            pltpu.VMEM((blocks, total, width), BF16),
            pltpu.VMEM((side,) + quarter.shape, BF16),
            pltpu.SemaphoreType.DMA((16 + blocks,)),
            pltpu.SemaphoreType.DMA((4 * side + 4 + blocks // 2,)),
        ],
        compiler_params=params(BIG_VMEM),
        cost_estimate=pl.CostEstimate(
            flops=10 * total * hidden * blocks * width,
            bytes_accessed=4 * rows.size + 4 * gate.size + 6 * total * hidden,
            transcendentals=total * hidden,
        ),
        name="expert",
    )(me, rows, d_act, gate, up, down)


def down_grad_kernel(act_ref, tan_ref, grad_ref):
    tangent = wide_rows(tan_ref)
    grad_ref[...] = lax.dot_general(
        act_ref[...], tangent, (((0,), (0,)), ((), ())), preferred_element_type=F32
    ).astype(BF16)


def down_grad(act, tangent):
    blocks, total, width = tangent.shape
    hidden = act.shape[1]
    return pl.pallas_call(
        down_grad_kernel,
        out_shape=jax.ShapeDtypeStruct((hidden, blocks * width), BF16),
        compiler_params=params(),
        cost_estimate=pl.CostEstimate(
            flops=2 * total * hidden * blocks * width,
            bytes_accessed=2 * tangent.size + 2 * total * hidden + 2 * hidden * blocks * width,
            transcendentals=0,
        ),
        name="down_grad",
    )(act, tangent)


def quarter_sum_kernel(in_ref, out_ref):
    for b in range(out_ref.shape[0]):
        total = in_ref[0, b].astype(F32)
        for s in range(1, in_ref.shape[0]):
            total = total + in_ref[s, b].astype(F32)
        out_ref[b] = total.astype(BF16)


def quarter_sum(parts):
    return pl.pallas_call(
        quarter_sum_kernel,
        out_shape=jax.ShapeDtypeStruct(parts.shape[1:], BF16),
        compiler_params=params(),
        name="quarter_sum",
    )(parts)


def half_sum_kernel(me_ref, *refs):
    count = len(refs) // 2
    for d in range(count):
        x = lax.rem(me_ref[0] + d, count)
        total = refs[0][x].astype(F32)
        for r in refs[1:count]:
            total = total + r[x].astype(F32)
        refs[count + d][...] = total.astype(BF16)


def half_sum(me, parts):
    vmem = pl.BlockSpec(memory_space=pltpu.VMEM)
    return pl.pallas_call(
        half_sum_kernel,
        in_specs=[pl.BlockSpec(memory_space=pltpu.SMEM)] + [vmem] * len(parts),
        out_shape=(jax.ShapeDtypeStruct(parts[0].shape[1:], BF16),) * len(parts),
        compiler_params=params(),
        name="half_sum",
    )(me, *parts)


def last_sum_kernel(out_ref, *refs):
    both_ref = refs[-1]
    width = out_ref.shape[2]
    total = out_ref[0].astype(F32)
    for s in range(1, out_ref.shape[0]):
        total = total + out_ref[s].astype(F32)
    both_ref[:, 0:width] = total.astype(BF16)
    total = refs[0][...].astype(F32)
    for r in refs[1:-1]:
        total = total + r[...].astype(F32)
    both_ref[:, width : 2 * width] = total.astype(BF16)


def last_sum(out_parts, grad_parts):
    _, total, width = out_parts.shape
    return pl.pallas_call(
        last_sum_kernel,
        out_shape=jax.ShapeDtypeStruct((total, 2 * width), BF16),
        compiler_params=params(),
        name="last_sum",
    )(out_parts, *grad_parts)


def combine_kernel(places_ref, weight_ref, back_ref, hid_ref, cot_ref, out_ref, grad_ref):
    block, width = hid_ref.shape
    slots = places_ref.shape[1]
    first = pl.program_id(0) * block
    where = lax.broadcasted_iota(jnp.int32, (block, slots), 0) + first
    picks = jnp.where(where == places_ref[...], 1.0, 0.0).astype(BF16)
    weighted = back_ref[:, 0:width].astype(F32) * weight_ref[...]
    terms = jnp.concatenate([weighted.astype(BF16), back_ref[:, width : 2 * width]], axis=1)
    sums = jnp.dot(picks, terms, preferred_element_type=F32)
    out_ref[...] = (hid_ref[...].astype(F32) + sums[:, 0:width]).astype(BF16)
    grad_ref[...] = (cot_ref[...].astype(F32) + sums[:, width : 2 * width]).astype(BF16)


def combine(places, weight, back, hidden, cotangent):
    length, width = hidden.shape
    slots = places.shape[1]
    block = 1024
    row_block = pl.BlockSpec((block, width), lambda i: (i, 0))

    def whole(shape):
        return pl.BlockSpec(shape, lambda i: (0, 0))

    return pl.pallas_call(
        combine_kernel,
        grid=(length // block,),
        in_specs=[
            whole((1, slots)),
            whole((slots, 1)),
            whole((slots, 2 * width)),
            row_block,
            row_block,
        ],
        out_specs=(row_block, row_block),
        out_shape=(jax.ShapeDtypeStruct(hidden.shape, BF16),) * 2,
        compiler_params=params(),
        name="combine",
    )(places, weight, back, hidden, cotangent)


def take_rows(array, index):
    return array.at[index].get(mode="promise_in_bounds")


def shift(block, dx, dy):
    side = SIDE
    moves = [
        (x * side + y, (x + dx) % side * side + (y + dy) % side)
        for x in range(side)
        for y in range(side)
    ]
    return lax.ppermute(block, "sp", moves)


def on_device(
    queries,
    keys,
    values,
    residual,
    cotangent,
    gate_proj,
    up_proj,
    down_proj,
    chosen,
    counts,
    route_weight,
):
    rows = queries.shape[0]
    length, width = residual.shape
    places = chosen[0]
    experts = places.shape[0]
    slots = experts * SLOTS
    group = lax.axis_size("sp")
    side = SIDE
    x_groups = [[x * side + y for x in range(side)] for y in range(side)]
    y_groups = [[x * side + y for y in range(side)] for x in range(side)]
    x_me = (lax.axis_index("sp") // side).reshape(1)
    y_me = (lax.axis_index("sp") % side).reshape(1)

    packed = pack(queries, keys, values)
    packed, cotangent_now, residual_now, flat, counts, route_weight = lax.optimization_barrier(
        (packed, cotangent, residual, places.reshape(slots), counts, route_weight)
    )
    qkv = lax.all_to_all(packed, "sp", split_axis=0, concat_axis=0, tiled=True)

    live = jnp.arange(SLOTS, dtype=jnp.int32)[None, :] < counts[0][:, None]
    weight = jnp.where(live, route_weight[0], jnp.float32(0.0)).reshape(slots, 1)
    picked_residual = take_rows(residual_now, flat)
    tangent = (take_rows(cotangent_now, flat).astype(F32) * weight).astype(BF16)
    all_tangents = lax.all_gather(tangent.reshape(experts, SLOTS, width), "ep", axis=0)
    own_tangents = lax.dynamic_index_in_dim(all_tangents, lax.axis_index("ep"), 1, False)
    own_tangents = own_tangents.reshape(-1, width)
    qkv, picked_residual = lax.optimization_barrier((qkv, picked_residual))
    owned_tangent = lax.all_gather(own_tangents, "sp", axis=0)

    query_rows = (flat // rows) * (3 * rows) + flat % rows
    picked_queries = take_rows(qkv.reshape(-1, HD), query_rows)
    block = min(512, slots)
    picked_hidden = attention(
        picked_queries,
        pl.BlockSpec((block, HD), lambda i: (i, 0)),
        picked_residual,
        0,
        slots,
        qkv,
        block,
        "picked_attention",
    )
    def full_attention(first, count, queries_here):
        return attention(
            queries_here,
            pl.BlockSpec((2, rows, HD), lambda i: (i + first, 0, 0)),
            residual,
            first,
            count * 2 * rows,
            qkv,
            2 * rows,
            "full_attention",
        )

    to_rows = jnp.broadcast_to(
        picked_hidden.reshape(experts, 1, SLOTS, width), (experts, side, SLOTS, width)
    )
    owned = lax.all_to_all(
        to_rows.reshape(-1, SLOTS, width),
        ("ep", "sp"),
        split_axis=0,
        concat_axis=0,
        axis_index_groups=[
            [e * group + x * side + y for e in range(experts) for y in range(side)]
            for x in range(side)
        ],
        tiled=True,
    )
    half = group // 4
    owned, queries_now = lax.optimization_barrier((owned, qkv))
    copies = jnp.broadcast_to(owned[None], (side,) + owned.shape)
    owned_rows = lax.all_to_all(
        copies.reshape(side, -1, width),
        "sp",
        split_axis=0,
        concat_axis=0,
        axis_index_groups=x_groups,
        tiled=True,
    ).reshape(side, experts, side, SLOTS, width)
    hidden_first = full_attention(0, half, queries_now)
    gate, up, down = gate_proj[0], up_proj[0], down_proj[0]
    d_act = tangent_product(owned_tangent, down)
    owned_rows, d_act, hidden_first, weight = lax.optimization_barrier(
        (owned_rows, d_act, hidden_first, weight)
    )
    act, out_part, *grad_parts = expert(y_me, owned_rows, d_act, gate, up, down)

    act, out_part, queries_now = lax.optimization_barrier((act, out_part, qkv))
    out_part = lax.all_to_all(
        out_part.reshape(side, -1, width),
        "sp",
        split_axis=0,
        concat_axis=0,
        axis_index_groups=x_groups,
        tiled=True,
    )
    grad_parts = [grad_parts[0]] + [shift(grad_parts[d], 0, d) for d in range(1, side)]
    grad_down = down_grad(act, owned_tangent)
    hidden_second = full_attention(half, half, queries_now)
    out_part, grad_down, hidden_second = lax.optimization_barrier(
        (out_part, grad_down, hidden_second)
    )
    out_part = quarter_sum(out_part.reshape(side, side, -1, width))
    out_part = lax.all_to_all(
        out_part, "sp", split_axis=0, concat_axis=0, axis_index_groups=y_groups, tiled=True
    )
    grad_parts = half_sum(x_me, grad_parts)
    grad_parts = [grad_parts[0]] + [shift(grad_parts[d], d, 0) for d in range(1, side)]
    back = last_sum(out_part, grad_parts).reshape(-1, SLOTS, 2 * width)
    back = lax.all_to_all(back, "ep", split_axis=0, concat_axis=0, tiled=True)
    block_out, grad_hidden = combine(
        flat.reshape(1, slots),
        weight,
        back.reshape(slots, 2 * width),
        jnp.concatenate([hidden_first, hidden_second], axis=0),
        cotangent,
    )
    return (block_out, grad_hidden, grad_down[None])


def solution(mesh):
    in_specs = (
        P(("ep", "sp"), None),
        P(("ep", "sp"), None),
        P(("ep", "sp"), None),
        P("ep", "sp"),
        P("ep", "sp"),
        P("ep", None, "sp"),
        P("ep", None, "sp"),
        P("ep", "sp", None),
        P("ep", None, None),
        P("ep", None),
        P("ep", None, None),
    )
    out_specs = (P("ep", "sp"), P("ep", "sp"), P("ep", "sp", None))
    return jax.shard_map(
        on_device, mesh=mesh, in_specs=in_specs, out_specs=out_specs, check_vma=False
    )
```
